32 devices in a mesh: groups: 2 (over y), seq: 8 (over z, core), fsdp: 2 (over x).
Axes of the slice: x: 2, y: 2, z: 4, core: 2. Of those that a mesh axis runs over, the one named last changes fastest.
Arguments:
- query_rows: bfloat16 [4096, 2048], P(('groups', 'seq'), 'fsdp'), parts along dimension 0, may hold values from -6 to 6
- key_rows: bfloat16 [4096, 2048], P(('groups', 'seq'), 'fsdp'), parts along dimension 0, may hold values from -6 to 6
- value_rows: bfloat16 [4096, 2048], P(('groups', 'seq'), 'fsdp'), parts along dimension 0, may hold values from -6 to 6
- out_weight: bfloat16 [2048, 2048], P('fsdp', 'seq'), may hold values from -0.125 to 0.125
- out_grad: bfloat16 [4096, 2048], P(('groups', 'seq')), parts along dimension 0, may hold values from -6 to 6
Outputs:
- mixed: bfloat16 [4096, 2048], P(('groups', 'seq')), parts along dimension 0
- query_grad: bfloat16 [4096, 2048], P(('groups', 'seq'), 'fsdp'), parts along dimension 0
- key_grad: bfloat16 [4096, 2048], P(('groups', 'seq'), 'fsdp'), parts along dimension 0
- value_grad: bfloat16 [4096, 2048], P(('groups', 'seq'), 'fsdp'), parts along dimension 0
- weight_grad: float32 [4096, 2048], P(('groups', 'fsdp'), 'seq'), parts along dimension 0
The draws below stay inside these ranges and needn't reach their ends.
There are 2 independent parts, one for each index of `groups`. The reference program is written for one: setup_inputs(seed, part) draws one part's arguments, and reference() takes and returns one part's arrays. A program takes and returns all parts, laid end to end along the dimension named above; an argument that names none is the same for every part. Nothing has to cross between parts.
All inputs are finite; a program needn't handle non-finite values.
Results may differ from the reference program's by a relative error of at most 0.013.
Values may be sent and summed in bfloat16 or wider, within the bound.
A program may use at most 128 MiB of HBM per device.

```python
import math
import jax
import jax.numpy as jnp
from jax import lax

D = 2048
HEADS = 16
HD = 128
TOK_DEV = 256
TOKENS = 2048


def spiked(drawn, rng, source, target, shards_of, factor):
    owner, partner = [(jnp.arange(drawn.shape[axis_at]) // (drawn.shape[axis_at] // shards_of)).reshape([-1 if axis == axis_at else 1 for axis in range(drawn.ndim)]) for axis_at in (source, target)]
    chosen = jax.random.permutation(rng, shards_of)[partner]
    strong = (owner == chosen) | (owner == (partner + shards_of // 2) % shards_of)
    return jnp.where(strong, factor * drawn, drawn)


def level_of(own_key, extent, cuts, low, largest):
    factor_of = 1.0
    for dim, parts in cuts:
        steps = jax.random.uniform(jax.random.fold_in(jax.random.fold_in(own_key, 6), dim), (parts,), jnp.float32, low / len(cuts), largest / len(cuts))
        factor_of = factor_of * jnp.repeat(jnp.exp(steps), extent[dim] // parts).reshape((-1,) + (1,) * (len(extent) - 1 - dim))
    return factor_of


def noise(key, dims, spread, bound, cuts=(), kind=jnp.bfloat16):
    gain = level_of(key, dims, cuts, -0.22, 0.18) if cuts else 1.0
    result = jax.random.normal(key, dims, jnp.float32) * spread * gain
    return jnp.minimum(jnp.maximum(result, -bound), bound).astype(kind)


def bell_draw_with(rng, dims, scale, most, pieces, heavy, kind=jnp.bfloat16):
    array = scale * jax.random.normal(rng, dims, jnp.float32)
    if pieces:
        array = array * level_of(rng, dims, pieces, -0.22, 0.18)
    return jnp.clip(spiked(array, jax.random.fold_in(rng, 3), *heavy), -most, most).astype(kind)


def setup_inputs(seed: int = 0, part: int = 0) -> dict:
    splits = jax.random.split(jax.random.key(seed), 6)
    own_keys = jax.random.split(jax.random.fold_in(splits[5], part), 6)
    return {
        "query_rows": noise(own_keys[0], (TOKENS, HEADS * HD), 1.0, 6.0, ((0, 8), (1, 2))),
        "key_rows": noise(own_keys[1], (TOKENS, HEADS * HD), 1.0, 6.0, ((0, 8), (1, 2))),
        "value_rows": noise(own_keys[2], (TOKENS, HEADS * HD), 1.0, 6.0, ((0, 8), (1, 2))),
        "out_weight": noise(splits[3], (HEADS * HD, D), (HEADS * HD) ** -0.5, 0.125, ((0, 2), (1, 8))),
        "out_grad": bell_draw_with(own_keys[4], (TOKENS, D), 1.0, 6.0, ((0, 8),), (0, 1, 8, 2.0)),
    }


HIGH = lax.Precision.HIGHEST

def reference(query_rows, key_rows, value_rows, out_weight, out_grad):
    factor = 1.0 / math.sqrt(HD * TOKENS)
    blocks = TOKENS // TOK_DEV

    def split(matrix):
        return matrix.reshape(blocks, TOK_DEV, HEADS, HD)
    queries, keys, values = (split(query_rows), split(key_rows), split(value_rows))
    positions = jnp.arange(TOK_DEV)
    causal = positions[:, None] >= positions[None, :]

    def masked(left, right):
        product = jnp.einsum('thd,shd->hts', left.astype(jnp.float32), right.astype(jnp.float32), precision=HIGH) * factor
        return jnp.where(causal, product, 0.0).astype(jnp.bfloat16)

    def forward_step(state, block):
        query_block, key_block, value_block = block
        scores = masked(query_block, key_block)
        within = jnp.einsum('hts,shd->thd', scores.astype(jnp.float32), value_block.astype(jnp.float32), precision=HIGH)
        carried = jnp.einsum('thd,hde->the', query_block.astype(jnp.float32), state, precision=HIGH) * factor
        attended = (within + carried).astype(jnp.bfloat16)
        growth = jnp.einsum('thd,the->hde', key_block.astype(jnp.float32), value_block.astype(jnp.float32), precision=HIGH)
        return (state + growth, (attended, state))
    zeros = jnp.zeros((HEADS, HD, HD), jnp.float32)
    _, (attended_blocks, prefixes) = lax.scan(forward_step, zeros, (queries, keys, values))
    attention = attended_blocks.reshape(TOKENS, HEADS * HD)
    mixed = jnp.dot(attention, out_weight, preferred_element_type=jnp.float32).astype(jnp.bfloat16)
    attn_grad = lax.dot_general(out_grad, out_weight, (((1,), (1,)), ((), ())), preferred_element_type=jnp.float32).astype(jnp.bfloat16)
    weight_grad = lax.dot_general(attention, out_grad, (((0,), (0,)), ((), ())), preferred_element_type=jnp.float32) / math.sqrt(TOKENS)
    grads = split(attn_grad)

    def backward_step(later, block):
        query_block, key_block, value_block, grad_block, prefix = block
        scores = masked(query_block, key_block)
        mixing = masked(grad_block, value_block)
        query_f = query_block.astype(jnp.float32)
        key_f = key_block.astype(jnp.float32)
        value_f = value_block.astype(jnp.float32)
        grad_f = grad_block.astype(jnp.float32)
        mixing_f = mixing.astype(jnp.float32)
        query_out = jnp.einsum('hts,shd->thd', mixing_f, key_f, precision=HIGH) + factor * jnp.einsum('the,hde->thd', grad_f, prefix, precision=HIGH)
        key_out = jnp.einsum('hts,thd->shd', mixing_f, query_f, precision=HIGH) + factor * jnp.einsum('the,hde->thd', value_f, later, precision=HIGH)
        value_out = jnp.einsum('hts,the->she', scores.astype(jnp.float32), grad_f, precision=HIGH) + factor * jnp.einsum('thd,hde->the', key_f, later, precision=HIGH)
        growth = jnp.einsum('thd,the->hde', query_f, grad_f, precision=HIGH)
        outputs = (query_out.astype(jnp.bfloat16), key_out.astype(jnp.bfloat16), value_out.astype(jnp.bfloat16))
        return (later + growth, outputs)
    _, (query_blocks, key_blocks, value_blocks) = lax.scan(backward_step, zeros, (queries, keys, values, grads, prefixes), reverse=True)
    query_grad = query_blocks.reshape(TOKENS, HEADS * HD)
    key_grad = key_blocks.reshape(TOKENS, HEADS * HD)
    value_grad = value_blocks.reshape(TOKENS, HEADS * HD)
    return (mixed, query_grad, key_grad, value_grad, weight_grad)
```

```python
import functools
import math

import jax
import jax.numpy as jnp
from jax import lax
from jax.experimental import pallas as pl
from jax.experimental.pallas import tpu as pltpu
from jax.sharding import PartitionSpec as P

HD = 128


HIGH = lax.Precision.HIGHEST


MESH = pl.DeviceIdType.MESH
BF = jnp.bfloat16
F32 = jnp.float32
CHUNKS = 4


def mm(a, b, dims):
    return lax.dot_general(a, b, ((dims[0], dims[1]), ((), ())), preferred_element_type=F32)


NN = ((1,), (0,))
NT = ((1,), (1,))
TN = ((0,), (0,))


def message_ids(nz):
    ids = {}

    def add(*name):
        ids[name] = len(ids)

    for d in range(1, nz):
        for way in ("up", "dn"):
            for kind in ("z", "y", "s", "ys"):
                add("w", kind, way, d)
    add("w", "own")
    for t in range(nz):
        add("og", t)
    for name in ("S", "T", "att", "pre", "pres", "suf", "sufs"):
        add(name)
    for t in range(nz):
        for r in range(CHUNKS):
            add("r", "up", t, r)
            add("r", "dn", t, r)
    for j in range(2 * nz):
        add("mix", j)
    return ids


def kernel(
    nz, ids, factor, grad_factor,
    q, k, v, w, og,
    mixed, qg, kg, vg, wg,
    wf, og_chip, att, s_own, s_sib, t_own, t_sib,
    pre_in, pre_sib, pre_out, suf_in, suf_sib, suf_out,
    prefix, sc, grads, acc, kg32, vg32, m, up_in, up_out, dn_in, dn_out, mix_out, mix_in,
    send, recv,
):
    length, width = q.shape
    heads = width // HD
    half = heads // 2
    hrows = width // 2
    cols = w.shape[1]
    rows = width // CHUNKS
    g = lax.axis_index("groups")
    s = lax.axis_index("seq")
    f = lax.axis_index("fsdp")
    z = lax.div(s, 2)
    c = lax.rem(s, 2)
    o = 1 - c
    sib = {"seq": z * 2 + o}
    upper = {"seq": s + 2}
    lower = {"seq": s - 2}
    ypart = {"groups": 1 - g}
    xpart = {"fsdp": 1 - f}
    last = nz - 1

    def make(name, src, dst, to):
        i = ids[name]
        return pltpu.make_async_remote_copy(
            src_ref=src, dst_ref=dst, send_sem=send.at[i], recv_sem=recv.at[i],
            device_id=to, device_id_type=MESH,
        )

    started = []

    def go(name, src, dst, to, cond=None):
        started.append((name, src, dst, to, cond))
        if cond is None:
            make(name, src, dst, to).start()
        else:
            @pl.when(cond)
            def _():
                make(name, src, dst, to).start()

    def got(name, dst, to, src=None):
        make(name, dst if src is None else src, dst, to).wait_recv()

    def hs(h):
        return slice(h * HD, (h + 1) * HD)

    for h in range(heads):
        s_own[h] = mm(k[:, hs(h)], v[:, hs(h)], TN).astype(BF)

    barrier = pltpu.get_barrier_semaphore()
    for to in (sib, ypart, xpart):
        pl.semaphore_signal(barrier, inc=1, device_id=to, device_id_type=MESH)

    @pl.when(z > 0)
    def _():
        pl.semaphore_signal(barrier, inc=1, device_id=lower, device_id_type=MESH)

    @pl.when(z < last)
    def _():
        pl.semaphore_signal(barrier, inc=1, device_id=upper, device_id_type=MESH)

    pl.semaphore_wait(barrier, 3 + (z > 0).astype(jnp.int32) + (z < last).astype(jnp.int32))

    def wslot(chip, core, h):
        return wf.at[chip * 2 + core, pl.ds(pl.multiple_of(h * hrows, hrows), hrows)]

    go(("S",), s_own, s_sib, sib)
    mine = w.at[pl.ds(pl.multiple_of(g * hrows, hrows), hrows)]
    go(("w", "z", "up", 1), mine, wslot(z, c, g), upper, z < last)
    go(("w", "z", "dn", 1), mine, wslot(z, c, g), lower, z > 0)
    go(("w", "own"), w, wf.at[s], sib)
    for t in range(nz):
        theirs = pl.ds(pl.multiple_of((2 * t + o) * cols, cols), cols)
        go(
            ("og", t), og.at[:, theirs],
            og_chip.at[pl.ds(pl.multiple_of(c * length, length), length), t * cols:(t + 1) * cols],
            sib,
        )
    wf[s] = w[...]
    own_rows = pl.ds(pl.multiple_of(c * length, length), length)
    for t in range(nz):
        own = pl.ds(pl.multiple_of((2 * t + c) * cols, cols), cols)
        og_chip[own_rows, t * cols:(t + 1) * cols] = og[:, own]

    lo = pl.multiple_of(c * half, half)
    mine_h = pl.ds(lo, half)

    def chain(name, out, own, other, buf_in, buf_sib, ok_in, ok_out, to):
        @pl.when(ok_in)
        def _():
            got((name,), buf_in, sib)
            out[...] = (
                buf_in[...].astype(F32) + own[mine_h].astype(F32) + other[mine_h].astype(F32)
            ).astype(BF)

        @pl.when(jnp.logical_not(ok_in))
        def _():
            out[...] = (own[mine_h].astype(F32) + other[mine_h].astype(F32)).astype(BF)

        go((name,), out, buf_in, to, ok_out)
        go((name + "s",), buf_in, buf_sib, sib, ok_in)

    def w_step(d):
        for way, ok, more, chip, to in (
            ("up", z >= d, z < last, z - d, upper),
            ("dn", z + d <= last, z > 0, z + d, lower),
        ):
            place = wslot(chip, c, g)

            @pl.when(ok)
            def _():
                got(("w", "z", way, d), place, sib)
            if d < last:
                go(("w", "z", way, d + 1), place, place, to, jnp.logical_and(ok, more))
            go(("w", "y", way, d), place, place, ypart, ok)
            go(("w", "s", way, d), place, place, sib, ok)

    def w_y(d):
        for way, ok, chip in (("up", z >= d, z - d), ("dn", z + d <= last, z + d)):
            place = wslot(chip, c, 1 - g)

            @pl.when(ok)
            def _():
                got(("w", "y", way, d), place, sib)
            go(("w", "ys", way, d), place, place, sib, ok)

    def w_sib():
        got(("w", "own"), wf.at[z * 2 + o], sib)
        for d in range(1, nz):
            for way, ok, chip in (("up", z >= d, z - d), ("dn", z + d <= last, z + d)):
                @pl.when(ok)
                def _():
                    got(("w", "s", way, d), wslot(chip, o, g), sib)
                    got(("w", "ys", way, d), wslot(chip, o, 1 - g), sib)

    got(("S",), s_sib, sib)
    chain("pre", pre_out, s_own, s_sib, pre_in, pre_sib, z > 0, z < last, upper)
    w_step(1)

    def joined(buf_in, buf_sib, other, ok, name, with_sib, out):
        @pl.when(ok)
        def _():
            got((name + "s",), buf_sib, sib)
            add = jnp.where(with_sib, 1.0, 0.0).astype(F32)
            out[mine_h] = (buf_in[...].astype(F32) + add * other[mine_h].astype(F32)).astype(BF)
            theirs_h = pl.ds(pl.multiple_of(o * half, half), half)
            out[theirs_h] = (buf_sib[...].astype(F32) + add * other[theirs_h].astype(F32)).astype(BF)

        @pl.when(jnp.logical_not(ok))
        def _():
            add = jnp.where(with_sib, 1.0, 0.0).astype(F32)
            out[...] = (add * other[...].astype(F32)).astype(BF)

    joined(pre_in, pre_sib, s_sib, z > 0, "pre", c == 1, prefix)
    causal = lax.broadcasted_iota(jnp.int32, (length, length), 0) >= lax.broadcasted_iota(
        jnp.int32, (length, length), 1
    )

    for h in range(heads):
        qh, kh, vh = q[:, hs(h)], k[:, hs(h)], v[:, hs(h)]
        scores = jnp.where(causal, mm(qh, kh, NT) * factor, 0.0).astype(BF)
        sc[h] = scores
        out = mm(scores, vh, NN) + mm(qh, prefix[h], NN) * factor
        att[own_rows, hs(h)] = out.astype(BF)
    go(("att",), att.at[own_rows], att.at[own_rows], sib)
    w_y(1)
    w_step(2) if nz > 2 else None

    sib_rows = pl.ds(pl.multiple_of(o * length, length), length)
    got(("att",), att.at[sib_rows], sib)
    for t in range(nz):
        got(("og", t), og_chip.at[sib_rows, t * cols:(t + 1) * cols], sib)
    for r in range(CHUNKS):
        m[r * rows:(r + 1) * rows] = (
            mm(att[:, r * rows:(r + 1) * rows], og_chip[...], TN) * grad_factor
        )

    def rs(way, t, r, origin):
        rr = slice(r * rows, (r + 1) * rows)
        buf_in, buf_out = (up_in, up_out) if way == "up" else (dn_in, dn_out)
        to = upper if way == "up" else lower
        first = z == 0 if way == "up" else z == last
        ahead = z < t if way == "up" else z > t
        tc = slice(t * cols, (t + 1) * cols)
        name = ("r", way, t, r)
        if origin:
            ok = jnp.logical_and(first, ahead)

            @pl.when(ok)
            def _():
                buf_out[t, rr] = m[rr, tc].astype(BF)
        else:
            ok = jnp.logical_and(jnp.logical_not(first), ahead)

            @pl.when(ok)
            def _():
                got(name, buf_in.at[t, rr], sib)
                buf_out[t, rr] = (m[rr, tc] + buf_in[t, rr].astype(F32)).astype(BF)
        go(name, buf_out.at[t, rr], buf_in.at[t, rr], to, ok)

    def rs_round(i, origin):
        for r in range(CHUNKS):
            rs("up", last - i, r, origin)
            rs("dn", i, r, origin)

    for i in range(nz - 1):
        rs_round(i, True)
    for d in range(2, nz):
        w_y(d)
        if d + 1 < nz:
            w_step(d + 1)
    w_sib()

    for j in range(2 * nz):
        part = mm(og[:, j * cols:(j + 1) * cols], wf[j], NT)
        if j == 0:
            acc[...] = part
        else:
            acc[...] += part
    grads[...] = acc[...].astype(BF)
    for h in range(heads):
        t_own[h] = mm(q[:, hs(h)], grads[:, hs(h)], TN).astype(BF)
    go(("T",), t_own, t_sib, sib)
    for j in range(2 * nz):
        mix_out[j] = mm(att[own_rows, :], wf[j], NN).astype(BF)
        go(("mix", j), mix_out.at[j], mix_in.at[j], xpart)
    got(("T",), t_sib, sib)
    rs_round(0, False)
    chain("suf", suf_out, t_own, t_sib, suf_in, suf_sib, z < last, z > 0, lower)

    for h in range(heads):
        qh, kh, vh, gh = q[:, hs(h)], k[:, hs(h)], v[:, hs(h)], grads[:, hs(h)]
        mixing = jnp.where(causal, mm(gh, vh, NT) * factor, 0.0).astype(BF)
        qg[:, hs(h)] = (mm(mixing, kh, NN) + mm(gh, prefix[h], NT) * factor).astype(BF)
        kg32[:, hs(h)] = mm(mixing, qh, TN)
        vg32[:, hs(h)] = mm(sc[h], gh, TN)

    for i in range(1, nz - 1):
        rs_round(i, False)

    joined(suf_in, suf_sib, t_sib, z < last, "suf", c == 0, prefix)
    for h in range(heads):
        kh, vh = k[:, hs(h)], v[:, hs(h)]
        kg[:, hs(h)] = (kg32[:, hs(h)] + mm(vh, prefix[h], NT) * factor).astype(BF)
        vg[:, hs(h)] = (vg32[:, hs(h)] + mm(kh, prefix[h], NN) * factor).astype(BF)

    for j in range(2 * nz):
        got(("mix", j), mix_in.at[j], xpart)
        mixed[:, j * cols:(j + 1) * cols] = (
            mix_out[j].astype(F32) + mix_in[j].astype(F32)
        ).astype(BF)

    here = pl.ds(pl.multiple_of(z * cols, cols), cols)
    for r in range(CHUNKS):
        rr = slice(r * rows, (r + 1) * rows)
        wg[rr] = m[rr, here]
        for way, ok, buf in (("up", z > 0, up_in), ("dn", z < last, dn_in)):
            for t in range(nz):
                @pl.when(jnp.logical_and(ok, z == t))
                def _():
                    got(("r", way, t, r), buf.at[t, rr], sib)
                    wg[rr] += buf[t, rr].astype(F32)

    for name, src, dst, to, cond in started:
        if cond is None:
            make(name, src, dst, to).wait_send()
        else:
            @pl.when(cond)
            def _():
                make(name, src, dst, to).wait_send()


def fused(query_rows, key_rows, value_rows, out_weight, out_grad):
    length, width = query_rows.shape
    model = out_grad.shape[1]
    cols = out_weight.shape[1]
    nseq = lax.axis_size("seq")
    nz = nseq // 2
    total = length * nseq
    heads = width // HD
    half = heads // 2
    ids = message_ids(nz)
    state = (heads, HD, HD)
    hstate = (half, HD, HD)
    vm = pltpu.VMEM
    scratch = [
        vm((nseq, width, cols), BF), vm((2 * length, nz * cols), BF), vm((2 * length, width), BF),
        vm(state, BF), vm(state, BF), vm(state, BF), vm(state, BF),
        vm(hstate, BF), vm(hstate, BF), vm(hstate, BF), vm(hstate, BF), vm(hstate, BF), vm(hstate, BF),
        vm(state, BF), vm((heads, length, length), BF), vm((length, width), BF),
        vm((length, width), F32), vm((length, width), F32), vm((length, width), F32),
        vm((width, nz * cols), F32),
        vm((nz, width, cols), BF), vm((nz, width, cols), BF),
        vm((nz, width, cols), BF), vm((nz, width, cols), BF),
        vm((nseq, length, cols), BF), vm((nseq, length, cols), BF),
        pltpu.SemaphoreType.DMA((len(ids),)), pltpu.SemaphoreType.DMA((len(ids),)),
    ]
    block = jax.ShapeDtypeStruct((length, width), BF)
    spec = pl.BlockSpec(memory_space=pltpu.VMEM)
    return pl.pallas_call(
        functools.partial(
            kernel, nz, ids, 1.0 / math.sqrt(HD * total), 1.0 / math.sqrt(total)
        ),
        out_shape=(
            jax.ShapeDtypeStruct((length, model), BF), block, block, block,
            jax.ShapeDtypeStruct((width, cols), F32),
        ),
        in_specs=[spec] * 5,
        out_specs=(spec,) * 5,
        scratch_shapes=scratch,
        compiler_params=pltpu.CompilerParams(
            collective_id=0, has_side_effects=True, vmem_limit_bytes=52 * 2**20
        ),
    )(query_rows, key_rows, value_rows, out_weight, out_grad)


def prefix_2(value, axis, join, neutral, backward):
    count = lax.axis_size(axis)
    place = lax.axis_index(axis)
    ahead = count - 1 - place if backward else place
    gathered = lax.all_gather(value.astype(jnp.bfloat16), axis)
    state = jnp.zeros_like(value) + jnp.asarray(neutral, value.dtype)

    def one(lap, state):
        source = count - 1 - lap if backward else lap
        return join(state, lax.dynamic_index_in_dim(gathered, source, 0, False).astype(value.dtype))

    return lax.fori_loop(0, ahead, one, state)


def added(earlier, later):
    return jax.tree.map(lambda first, second: first + second, earlier, later)


def on_device(query_rows, key_rows, value_rows, out_weight, out_grad):
    length = query_rows.shape[0]
    width = query_rows.shape[1]
    heads_here = width // HD
    total = length * lax.axis_size("seq")
    factor = 1.0 / math.sqrt(HD * total)
    grad_factor = 1.0 / math.sqrt(total)
    queries = query_rows.reshape(length, heads_here, HD)
    keys = key_rows.reshape(length, heads_here, HD)
    values = value_rows.reshape(length, heads_here, HD)
    full_weight = lax.all_gather(out_weight, "seq", axis=1, tiled=True)
    attn_grad = lax.dot_general(
        out_grad, full_weight, (((1,), (1,)), ((), ())), preferred_element_type=jnp.float32
    ).astype(jnp.bfloat16)
    grads = attn_grad.reshape(length, heads_here, HD)
    own_state = jnp.einsum("thd,the->hde", keys, values, preferred_element_type=jnp.float32)
    own_grad_state = jnp.einsum("thd,the->hde", queries, grads, preferred_element_type=jnp.float32)
    zeros = jnp.zeros_like(own_state)
    prefix = prefix_2(own_state, "seq", added, zeros, False)
    suffix = prefix_2(own_grad_state, "seq", added, zeros, True)
    positions = jnp.arange(length)
    causal = positions[:, None] >= positions[None, :]
    raw_scores = (
        jnp.einsum("thd,shd->hts", queries, keys, preferred_element_type=jnp.float32) * factor
    )
    scores = jnp.where(causal, raw_scores, 0.0).astype(jnp.bfloat16)
    within = jnp.einsum("hts,shd->thd", scores, values, preferred_element_type=jnp.float32)
    carried = (
        jnp.einsum("thd,hde->the", queries.astype(jnp.float32), prefix, precision=HIGH) * factor
    )
    attention = (within + carried).astype(jnp.bfloat16).reshape(length, width)
    partial_out = jnp.dot(attention, full_weight, preferred_element_type=jnp.float32)
    mixed = lax.psum(partial_out.astype(jnp.bfloat16), "fsdp")
    weight_grad = lax.psum_scatter(
        lax.dot_general(
            out_grad, attention, (((0,), (0,)), ((), ())), preferred_element_type=jnp.float32
        )
        * grad_factor,
        "seq",
        scatter_dimension=0,
        tiled=True,
    ).T
    raw_mixing = (
        jnp.einsum("the,she->hts", grads, values, preferred_element_type=jnp.float32) * factor
    )
    mixing = jnp.where(causal, raw_mixing, 0.0).astype(jnp.bfloat16)
    query_grad = jnp.einsum(
        "hts,shd->thd", mixing, keys, preferred_element_type=jnp.float32
    ) + factor * jnp.einsum("the,hde->thd", grads.astype(jnp.float32), prefix, precision=HIGH)
    key_grad = jnp.einsum(
        "hts,thd->shd", mixing, queries, preferred_element_type=jnp.float32
    ) + factor * jnp.einsum("the,hde->thd", values.astype(jnp.float32), suffix, precision=HIGH)
    value_grad = jnp.einsum(
        "hts,the->she", scores, grads, preferred_element_type=jnp.float32
    ) + factor * jnp.einsum("thd,hde->the", keys.astype(jnp.float32), suffix, precision=HIGH)
    query_grad = query_grad.astype(jnp.bfloat16).reshape(length, width)
    key_grad = key_grad.astype(jnp.bfloat16).reshape(length, width)
    value_grad = value_grad.astype(jnp.bfloat16).reshape(length, width)
    return (mixed, query_grad, key_grad, value_grad, weight_grad)


def fits(mesh):
    shape = mesh.shape
    return (
        shape["groups"] == 2 and shape["fsdp"] == 2 and shape["seq"] % 2 == 0
        and 2 < shape["seq"] <= 8
    )


def solution(mesh):
    return jax.shard_map(
        fused if fits(mesh) else on_device,
        mesh=mesh,
        in_specs=(
            P(("groups", "seq"), "fsdp"),
            P(("groups", "seq"), "fsdp"),
            P(("groups", "seq"), "fsdp"),
            P("fsdp", "seq"),
            P(("groups", "seq"), None),
        ),
        out_specs=(
            P(("groups", "seq"), None),
            P(("groups", "seq"), "fsdp"),
            P(("groups", "seq"), "fsdp"),
            P(("groups", "seq"), "fsdp"),
            P(("groups", "fsdp"), "seq"),
        ),
        check_vma=False,
    )
```

```python
import functools
import math

import jax
import jax.numpy as jnp
from jax import lax
from jax.experimental import pallas as pl
from jax.experimental.pallas import tpu as pltpu
from jax.sharding import PartitionSpec as P

HD = 128


HIGH = lax.Precision.HIGHEST


MESH = pl.DeviceIdType.MESH
BF = jnp.bfloat16
F32 = jnp.float32
CHUNKS = 4


def mm(a, b, dims):
    return lax.dot_general(a, b, ((dims[0], dims[1]), ((), ())), preferred_element_type=F32)


NN = ((1,), (0,))
NT = ((1,), (1,))
TN = ((0,), (0,))


def message_ids(nz, half):
    ids = {}

    def add(*name):
        ids[name] = len(ids)

    for d in range(1, nz):
        for way in ("up", "dn"):
            for kind in ("z", "y", "s", "ys"):
                add("w", kind, way, d)
    add("w", "own")
    for t in range(nz):
        add("og", t)
    for name in ("S", "T", "att"):
        add(name)
    for name in ("pre", "pres", "suf", "sufs"):
        for h in range(half):
            add(name, h)
    for t in range(nz):
        for r in range(CHUNKS):
            add("r", "up", t, r)
            add("r", "dn", t, r)
    for d in range(nz):
        for way in ("up", "dn"):
            for core in (0, 1):
                add("mix", way, d, core)
    return ids


def kernel(
    nz, ids, factor, grad_factor,
    q, k, v, w, og,
    mixed, qg, kg, vg, wg,
    wf, og_chip, att, s_own, s_sib, t_own, t_sib,
    pre_in, pre_sib, pre_out, suf_in, suf_sib, suf_out,
    prefix, sc, grads, acc, kg32, vg32, m, up_in, up_out, dn_in, dn_out, mix_out, mix_in,
    send, recv,
):
    length, width = q.shape
    heads = width // HD
    half = heads // 2
    hrows = width // 2
    cols = w.shape[1]
    rows = width // CHUNKS
    g = lax.axis_index("groups")
    s = lax.axis_index("seq")
    f = lax.axis_index("fsdp")
    z = lax.div(s, 2)
    c = lax.rem(s, 2)
    o = 1 - c
    sib = {"seq": z * 2 + o}
    upper = {"seq": s + 2}
    lower = {"seq": s - 2}
    ypart = {"groups": 1 - g}
    xpart = {"fsdp": 1 - f}
    last = nz - 1

    def make(name, src, dst, to):
        i = ids[name]
        return pltpu.make_async_remote_copy(
            src_ref=src, dst_ref=dst, send_sem=send.at[i], recv_sem=recv.at[i],
            device_id=to, device_id_type=MESH,
        )

    started = []

    def go(name, src, dst, to, cond=None):
        started.append((name, src, dst, to, cond))
        if cond is None:
            make(name, src, dst, to).start()
        else:
            @pl.when(cond)
            def _():
                make(name, src, dst, to).start()

    def got(name, dst, to, src=None):
        make(name, dst if src is None else src, dst, to).wait_recv()

    def hs(h):
        return slice(h * HD, (h + 1) * HD)

    for h in range(heads):
        s_own[h] = mm(k[:, hs(h)], v[:, hs(h)], TN).astype(BF)

    barrier = pltpu.get_barrier_semaphore()
    for to in (sib, ypart, xpart):
        pl.semaphore_signal(barrier, inc=1, device_id=to, device_id_type=MESH)

    @pl.when(z > 0)
    def _():
        pl.semaphore_signal(barrier, inc=1, device_id=lower, device_id_type=MESH)

    @pl.when(z < last)
    def _():
        pl.semaphore_signal(barrier, inc=1, device_id=upper, device_id_type=MESH)

    pl.semaphore_wait(barrier, 3 + (z > 0).astype(jnp.int32) + (z < last).astype(jnp.int32))

    def wslot(chip, core, h):
        return wf.at[chip * 2 + core, pl.ds(pl.multiple_of(h * hrows, hrows), hrows)]

    go(("S",), s_own, s_sib, sib)
    mine = w.at[pl.ds(pl.multiple_of(g * hrows, hrows), hrows)]
    go(("w", "z", "up", 1), mine, wslot(z, c, g), upper, z < last)
    go(("w", "z", "dn", 1), mine, wslot(z, c, g), lower, z > 0)
    go(("w", "own"), w, wf.at[s], sib)
    for t in range(nz):
        theirs = pl.ds(pl.multiple_of((2 * t + o) * cols, cols), cols)
        go(
            ("og", t), og.at[:, theirs],
            og_chip.at[pl.ds(pl.multiple_of(c * length, length), length), t * cols:(t + 1) * cols],
            sib,
        )
    wf[s] = w[...]
    own_rows = pl.ds(pl.multiple_of(c * length, length), length)
    for t in range(nz):
        own = pl.ds(pl.multiple_of((2 * t + c) * cols, cols), cols)
        og_chip[own_rows, t * cols:(t + 1) * cols] = og[:, own]

    lo = pl.multiple_of(c * half, half)
    mine_h = pl.ds(lo, half)

    def origin(name, out, own, other, buf_in, ok_in, to):
        first = jnp.logical_not(ok_in)

        @pl.when(first)
        def _():
            out[...] = (own[mine_h].astype(F32) + other[mine_h].astype(F32)).astype(BF)

        for h in range(half):
            go((name, h), out.at[h], buf_in.at[h], to, first)

    def relay(name, out, own, other, buf_in, buf_sib, ok_in, ok_out, to):
        for h in range(half):
            @pl.when(ok_in)
            def _():
                got((name, h), buf_in.at[h], sib)
                out[h] = (
                    buf_in[h].astype(F32) + own[lo + h].astype(F32) + other[lo + h].astype(F32)
                ).astype(BF)
            go((name, h), out.at[h], buf_in.at[h], to, jnp.logical_and(ok_in, ok_out))
            go((name + "s", h), buf_in.at[h], buf_sib.at[h], sib, ok_in)

    def w_step(d):
        for way, ok, more, chip, to in (
            ("up", z >= d, z < last, z - d, upper),
            ("dn", z + d <= last, z > 0, z + d, lower),
        ):
            place = wslot(chip, c, g)

            @pl.when(ok)
            def _():
                got(("w", "z", way, d), place, sib)
            if d < last:
                go(("w", "z", way, d + 1), place, place, to, jnp.logical_and(ok, more))
            go(("w", "y", way, d), place, place, ypart, ok)
            go(("w", "s", way, d), place, place, sib, ok)

    def w_y(d):
        for way, ok, chip in (("up", z >= d, z - d), ("dn", z + d <= last, z + d)):
            place = wslot(chip, c, 1 - g)

            @pl.when(ok)
            def _():
                got(("w", "y", way, d), place, sib)
            go(("w", "ys", way, d), place, place, sib, ok)

    def shard(way, d, core, j, ok):
        jc = pl.ds(pl.multiple_of(j * cols, cols), cols)

        @pl.when(ok)
        def _():
            acc[...] += mm(og[:, jc], wf[j], NT)
            mix_out[j] = mm(att[own_rows, :], wf[j], NN).astype(BF)
        go(("mix", way, d, core), mix_out.at[j], mix_in.at[j], xpart, ok)

    def shards(d):
        for way, ok, chip in (("up", z >= d, z - d), ("dn", z + d <= last, z + d)):
            shard(way, d, 0, chip * 2 + c, ok)

            @pl.when(ok)
            def _():
                got(("w", "s", way, d), wslot(chip, o, g), sib)
                got(("w", "ys", way, d), wslot(chip, o, 1 - g), sib)
            shard(way, d, 1, chip * 2 + o, ok)

    causal = lax.broadcasted_iota(jnp.int32, (length, length), 0) >= lax.broadcasted_iota(
        jnp.int32, (length, length), 1
    )

    def joined(buf_in, buf_sib, other, ok, name, with_sib, out):
        @pl.when(ok)
        def _():
            for h in range(half):
                got((name + "s", h), buf_sib.at[h], sib)
            add = jnp.where(with_sib, 1.0, 0.0).astype(F32)
            out[mine_h] = (buf_in[...].astype(F32) + add * other[mine_h].astype(F32)).astype(BF)
            theirs_h = pl.ds(pl.multiple_of(o * half, half), half)
            out[theirs_h] = (buf_sib[...].astype(F32) + add * other[theirs_h].astype(F32)).astype(BF)

        @pl.when(jnp.logical_not(ok))
        def _():
            add = jnp.where(with_sib, 1.0, 0.0).astype(F32)
            out[...] = (add * other[...].astype(F32)).astype(BF)

    def m_step(r):
        m[r * rows:(r + 1) * rows] = (
            mm(att[:, r * rows:(r + 1) * rows], og_chip[...], TN) * grad_factor
        )

    def rs(way, t, r, origin):
        rr = slice(r * rows, (r + 1) * rows)
        buf_in, buf_out = (up_in, up_out) if way == "up" else (dn_in, dn_out)
        to = upper if way == "up" else lower
        first = z == 0 if way == "up" else z == last
        ahead = z < t if way == "up" else z > t
        tc = slice(t * cols, (t + 1) * cols)
        name = ("r", way, t, r)
        if origin:
            ok = jnp.logical_and(first, ahead)

            @pl.when(ok)
            def _():
                buf_out[t, rr] = m[rr, tc].astype(BF)
        else:
            ok = jnp.logical_and(jnp.logical_not(first), ahead)

            @pl.when(ok)
            def _():
                got(name, buf_in.at[t, rr], sib)
                buf_out[t, rr] = (m[rr, tc] + buf_in[t, rr].astype(F32)).astype(BF)
        go(name, buf_out.at[t, rr], buf_in.at[t, rr], to, ok)

    def rs_round(r, origin):
        for i in range(nz - 1):
            rs("up", last - i, r, origin)
            rs("dn", i, r, origin)

    got(("S",), s_sib, sib)
    origin("pre", pre_out, s_own, s_sib, pre_in, z > 0, upper)
    for h in range(heads):
        scores = jnp.where(causal, mm(q[:, hs(h)], k[:, hs(h)], NT) * factor, 0.0).astype(BF)
        sc[h] = scores
        acc[:, hs(h)] = mm(scores, v[:, hs(h)], NN)
    relay("pre", pre_out, s_own, s_sib, pre_in, pre_sib, z > 0, z < last, upper)
    w_step(1)
    joined(pre_in, pre_sib, s_sib, z > 0, "pre", c == 1, prefix)
    for h in range(heads):
        att[own_rows, hs(h)] = (acc[:, hs(h)] + mm(q[:, hs(h)], prefix[h], NN) * factor).astype(BF)
    go(("att",), att.at[own_rows], att.at[own_rows], sib)
    acc[...] = jnp.zeros_like(acc)
    always = z >= 0
    shard("up", 0, 0, s, always)
    w_y(1)
    sib_rows = pl.ds(pl.multiple_of(o * length, length), length)
    got(("att",), att.at[sib_rows], sib)
    for t in range(nz):
        got(("og", t), og_chip.at[sib_rows, t * cols:(t + 1) * cols], sib)
    m_step(0)
    rs_round(0, True)
    w_step(2)
    for r in range(1, CHUNKS):
        m_step(r)
        rs_round(r, True)
    got(("w", "own"), wf.at[z * 2 + o], sib)
    shard("up", 0, 1, z * 2 + o, always)
    shards(1)
    w_y(2)
    rs_round(0, False)
    w_step(3)
    shards(2)
    w_y(3)
    shards(3)

    for h in range(heads):
        grads[:, hs(h)] = acc[:, hs(h)].astype(BF)
        t_own[h] = mm(q[:, hs(h)], grads[:, hs(h)], TN).astype(BF)
    go(("T",), t_own, t_sib, sib)
    rs_round(1, False)
    got(("T",), t_sib, sib)
    origin("suf", suf_out, t_own, t_sib, suf_in, z < last, lower)
    for h in range(heads):
        qh, kh, vh, gh = q[:, hs(h)], k[:, hs(h)], v[:, hs(h)], grads[:, hs(h)]
        mixing = jnp.where(causal, mm(gh, vh, NT) * factor, 0.0).astype(BF)
        qg[:, hs(h)] = (mm(mixing, kh, NN) + mm(gh, prefix[h], NT) * factor).astype(BF)
        kg32[:, hs(h)] = mm(mixing, qh, TN)
        vg32[:, hs(h)] = mm(sc[h], gh, TN)
    rs_round(2, False)
    relay("suf", suf_out, t_own, t_sib, suf_in, suf_sib, z < last, z > 0, lower)
    rs_round(3, False)

    joined(suf_in, suf_sib, t_sib, z < last, "suf", c == 0, prefix)
    for h in range(heads):
        kh, vh = k[:, hs(h)], v[:, hs(h)]
        kg[:, hs(h)] = (kg32[:, hs(h)] + mm(vh, prefix[h], NT) * factor).astype(BF)
        vg[:, hs(h)] = (vg32[:, hs(h)] + mm(kh, prefix[h], NN) * factor).astype(BF)

    for d in range(nz):
        for way, ok, chip in (("up", z >= d, z - d), ("dn", z + d <= last, z + d)):
            if d == 0 and way == "dn":
                continue
            for core, j in ((0, chip * 2 + c), (1, chip * 2 + o)):
                @pl.when(ok)
                def _():
                    got(("mix", way, d, core), mix_in.at[j], xpart)
                    jc = pl.ds(pl.multiple_of(j * cols, cols), cols)
                    mixed[:, jc] = (
                        mix_out[j].astype(F32) + mix_in[j].astype(F32)
                    ).astype(BF)

    here = pl.ds(pl.multiple_of(z * cols, cols), cols)
    for r in range(CHUNKS):
        rr = slice(r * rows, (r + 1) * rows)
        wg[rr] = m[rr, here]
        for way, ok, buf in (("up", z > 0, up_in), ("dn", z < last, dn_in)):
            for t in range(nz):
                @pl.when(jnp.logical_and(ok, z == t))
                def _():
                    got(("r", way, t, r), buf.at[t, rr], sib)
                    wg[rr] += buf[t, rr].astype(F32)

    for name, src, dst, to, cond in started:
        if cond is None:
            make(name, src, dst, to).wait_send()
        else:
            @pl.when(cond)
            def _():
                make(name, src, dst, to).wait_send()


def placed(*refs):
    n = len(refs) // 2
    for i in range(n):
        refs[n + i][...] = refs[i][...]


def fused(query_rows, key_rows, value_rows, out_weight, out_grad):
    length, width = query_rows.shape
    model = out_grad.shape[1]
    cols = out_weight.shape[1]
    nseq = lax.axis_size("seq")
    nz = nseq // 2
    total = length * nseq
    heads = width // HD
    half = heads // 2
    ids = message_ids(nz, half)
    state = (heads, HD, HD)
    hstate = (half, HD, HD)
    vm = pltpu.VMEM
    scratch = [
        vm((nseq, width, cols), BF), vm((2 * length, nz * cols), BF), vm((2 * length, width), BF),
        vm(state, BF), vm(state, BF), vm(state, BF), vm(state, BF),
        vm(hstate, BF), vm(hstate, BF), vm(hstate, BF), vm(hstate, BF), vm(hstate, BF), vm(hstate, BF),
        vm(state, BF), vm((heads, length, length), BF), vm((length, width), BF),
        vm((length, width), F32), vm((length, width), F32), vm((length, width), F32),
        vm((width, nz * cols), F32),
        vm((nz, width, cols), BF), vm((nz, width, cols), BF),
        vm((nz, width, cols), BF), vm((nz, width, cols), BF),
        vm((nseq, length, cols), BF), vm((nseq, length, cols), BF),
        pltpu.SemaphoreType.DMA((len(ids),)), pltpu.SemaphoreType.DMA((len(ids),)),
    ]
    block = jax.ShapeDtypeStruct((length, width), BF)
    spec = pl.BlockSpec(memory_space=pltpu.VMEM)
    results = pl.pallas_call(
        functools.partial(
            kernel, nz, ids, 1.0 / math.sqrt(HD * total), 1.0 / math.sqrt(total)
        ),
        out_shape=(
            jax.ShapeDtypeStruct((length, model), BF), block, block, block,
            jax.ShapeDtypeStruct((width, cols), F32),
        ),
        in_specs=[spec] * 5,
        out_specs=(spec,) * 5,
        scratch_shapes=scratch,
        compiler_params=pltpu.CompilerParams(
            collective_id=0, has_side_effects=True, vmem_limit_bytes=52 * 2**20
        ),
    )(query_rows, key_rows, value_rows, out_weight, out_grad)
    blocks = 4
    specs = [pl.BlockSpec((a.shape[0] // blocks, a.shape[1]), lambda i: (i, 0)) for a in results]
    return pl.pallas_call(
        placed,
        grid=(blocks,),
        out_shape=tuple(jax.ShapeDtypeStruct(a.shape, a.dtype) for a in results),
        in_specs=specs,
        out_specs=tuple(specs),
        compiler_params=pltpu.CompilerParams(vmem_limit_bytes=40 * 2**20),
    )(*results)


def prefix_2(value, axis, join, neutral, backward):
    count = lax.axis_size(axis)
    place = lax.axis_index(axis)
    ahead = count - 1 - place if backward else place
    gathered = lax.all_gather(value.astype(jnp.bfloat16), axis)
    state = jnp.zeros_like(value) + jnp.asarray(neutral, value.dtype)

    def one(lap, state):
        source = count - 1 - lap if backward else lap
        return join(state, lax.dynamic_index_in_dim(gathered, source, 0, False).astype(value.dtype))

    return lax.fori_loop(0, ahead, one, state)


def added(earlier, later):
    return jax.tree.map(lambda first, second: first + second, earlier, later)


def on_device(query_rows, key_rows, value_rows, out_weight, out_grad):
    length = query_rows.shape[0]
    width = query_rows.shape[1]
    heads_here = width // HD
    total = length * lax.axis_size("seq")
    factor = 1.0 / math.sqrt(HD * total)
    grad_factor = 1.0 / math.sqrt(total)
    queries = query_rows.reshape(length, heads_here, HD)
    keys = key_rows.reshape(length, heads_here, HD)
    values = value_rows.reshape(length, heads_here, HD)
    full_weight = lax.all_gather(out_weight, "seq", axis=1, tiled=True)
    attn_grad = lax.dot_general(
        out_grad, full_weight, (((1,), (1,)), ((), ())), preferred_element_type=jnp.float32
    ).astype(jnp.bfloat16)
    grads = attn_grad.reshape(length, heads_here, HD)
    own_state = jnp.einsum("thd,the->hde", keys, values, preferred_element_type=jnp.float32)
    own_grad_state = jnp.einsum("thd,the->hde", queries, grads, preferred_element_type=jnp.float32)
    zeros = jnp.zeros_like(own_state)
    prefix = prefix_2(own_state, "seq", added, zeros, False)
    suffix = prefix_2(own_grad_state, "seq", added, zeros, True)
    positions = jnp.arange(length)
    causal = positions[:, None] >= positions[None, :]
    raw_scores = (
        jnp.einsum("thd,shd->hts", queries, keys, preferred_element_type=jnp.float32) * factor
    )
    scores = jnp.where(causal, raw_scores, 0.0).astype(jnp.bfloat16)
    within = jnp.einsum("hts,shd->thd", scores, values, preferred_element_type=jnp.float32)
    carried = (
        jnp.einsum("thd,hde->the", queries.astype(jnp.float32), prefix, precision=HIGH) * factor
    )
    attention = (within + carried).astype(jnp.bfloat16).reshape(length, width)
    partial_out = jnp.dot(attention, full_weight, preferred_element_type=jnp.float32)
    mixed = lax.psum(partial_out.astype(jnp.bfloat16), "fsdp")
    weight_grad = lax.psum_scatter(
        lax.dot_general(
            out_grad, attention, (((0,), (0,)), ((), ())), preferred_element_type=jnp.float32
        )
        * grad_factor,
        "seq",
        scatter_dimension=0,
        tiled=True,
    ).T
    raw_mixing = (
        jnp.einsum("the,she->hts", grads, values, preferred_element_type=jnp.float32) * factor
    )
    mixing = jnp.where(causal, raw_mixing, 0.0).astype(jnp.bfloat16)
    query_grad = jnp.einsum(
        "hts,shd->thd", mixing, keys, preferred_element_type=jnp.float32
    ) + factor * jnp.einsum("the,hde->thd", grads.astype(jnp.float32), prefix, precision=HIGH)
    key_grad = jnp.einsum(
        "hts,thd->shd", mixing, queries, preferred_element_type=jnp.float32
    ) + factor * jnp.einsum("the,hde->thd", values.astype(jnp.float32), suffix, precision=HIGH)
    value_grad = jnp.einsum(
        "hts,the->she", scores, grads, preferred_element_type=jnp.float32
    ) + factor * jnp.einsum("thd,hde->the", keys.astype(jnp.float32), suffix, precision=HIGH)
    query_grad = query_grad.astype(jnp.bfloat16).reshape(length, width)
    key_grad = key_grad.astype(jnp.bfloat16).reshape(length, width)
    value_grad = value_grad.astype(jnp.bfloat16).reshape(length, width)
    return (mixed, query_grad, key_grad, value_grad, weight_grad)


def fits(mesh):
    shape = mesh.shape
    return (
        shape["groups"] == 2 and shape["fsdp"] == 2
        and shape["seq"] == 8
    )


def solution(mesh):
    return jax.shard_map(
        fused if fits(mesh) else on_device,
        mesh=mesh,
        in_specs=(
            P(("groups", "seq"), "fsdp"),
            P(("groups", "seq"), "fsdp"),
            P(("groups", "seq"), "fsdp"),
            P("fsdp", "seq"),
            P(("groups", "seq"), None),
        ),
        out_specs=(
            P(("groups", "seq"), None),
            P(("groups", "seq"), "fsdp"),
            P(("groups", "seq"), "fsdp"),
            P(("groups", "seq"), "fsdp"),
            P(("groups", "fsdp"), "seq"),
        ),
        check_vma=False,
    )
```
